32 devices in a mesh: section: 4 (over y, x), dp: 8 (over z, core).
Axes of the slice: x: 2, y: 2, z: 4, core: 2. Of those that a mesh axis runs over, the one named last changes fastest.
Arguments:
- inputs: bfloat16 [4, 256, 2048], P(None, 'dp'), may hold values from -6 to 6
- route: int32 [4, 4, 256, 6], P('section', None, 'dp'), may hold values from 0 to 7, as said below
- gain: bfloat16 [4, 2048], P('section'), may hold values from 0.099609375 to 1.8984375
- router: bfloat16 [4, 2048, 8], P('section'), may hold values from -0.125 to 0.125
- w_gate: bfloat16 [4, 8, 2048, 768], P('section', 'dp'), may hold values from -0.125 to 0.125
- w_up: bfloat16 [4, 8, 2048, 768], P('section', 'dp'), may hold values from -0.125 to 0.125
- w_down: bfloat16 [4, 8, 768, 2048], P('section', 'dp'), may hold values from -0.21875 to 0.21875
Outputs:
- states: bfloat16 [4, 4, 256, 2048], P('section', None, 'dp')
The draws below stay inside these ranges and needn't reach their ends.
Inputs may be any that keep to these rules, and one draw needn't show every extreme that they name: `route`: each token names 6 different experts. Among the 32 tokens of one index of dp in one micro-batch and layer, no expert is named more than 32 times; in every micro-batch and layer one expert is named exactly 32 times by the tokens of every index of dp.
All inputs are finite; a program needn't handle non-finite values.
Results may differ from the reference program's by a relative error of at most 0.015.
Values may be sent and summed in bfloat16 or wider, within the bound.
A program may use at most 128 MiB of HBM per device.

```python
import jax
import jax.numpy as jnp
from jax import lax

D = 2048
FF = 768
TOP = 6
TOK_DEV = 32
MICRO = 4
EXPERTS = 8
LAYERS = 4
TOKENS = 256
PAIR = 48
CAP = 32
LOW = 16
N_DP = 8


def search_loads(cumul, spots):
    return jnp.searchsorted(cumul, spots, side='right').astype(jnp.int32)


def shuffle_rows(key):
    return jax.random.permutation(key, TOK_DEV).astype(jnp.int32)


def route_table(key):
    perm_key, load_key, shuffle_key = jax.random.split(key, 3)
    perm = jax.random.permutation(perm_key, EXPERTS).astype(jnp.int32)
    first = jax.random.randint(load_key, (N_DP, EXPERTS // 2), LOW, CAP + 1, dtype=jnp.int32)
    first = first.at[:, 0].set(CAP)
    loads = jnp.stack([first, PAIR - first], axis=2).reshape(N_DP, EXPERTS)
    cumul = jnp.cumsum(loads, axis=1).astype(jnp.int32)
    spots = jnp.arange(TOK_DEV * TOP, dtype=jnp.int32)
    where_pos = jax.vmap(search_loads, in_axes=(0, None))(cumul, spots)
    sequence = perm[jnp.clip(where_pos, 0, EXPERTS - 1)]
    table = sequence.reshape(N_DP, TOP, TOK_DEV).transpose(0, 2, 1)
    shuffles = jax.vmap(shuffle_rows)(jax.random.split(shuffle_key, N_DP))
    table = jnp.take_along_axis(table, shuffles[:, :, None], axis=1)
    return table.reshape(TOKENS, TOP)


def draw_route(key, part):
    keys = jax.random.split(jax.random.fold_in(key, 17), LAYERS * MICRO)
    tables = jax.vmap(route_table)(keys)
    return tables.reshape(LAYERS, MICRO, TOKENS, TOP).astype(jnp.int32)


def shard_levels(own_key, dims, cuts, smallest, top_value):
    def one(dim, blocks):
        draws = jax.random.uniform(jax.random.fold_in(jax.random.fold_in(own_key, 6), dim), (blocks,), jnp.float32, smallest / len(cuts), top_value / len(cuts))
        return jnp.repeat(jnp.exp(draws), dims[dim] // blocks).reshape((-1,) + (1,) * (len(dims) - dim - 1))

    factor_of = one(*cuts[0])
    for cut in cuts[1:]:
        factor_of = factor_of * one(*cut)
    return factor_of


def centred(rng, shape, spread, bound, cuts=(), held_as=jnp.bfloat16):
    drawn = spread * jax.random.normal(rng, shape, jnp.float32)
    if cuts:
        drawn = drawn * shard_levels(rng, shape, cuts, -0.22, 0.18)
    return jnp.clip(drawn, -bound, bound).astype(held_as)


def setup_inputs(seed: int = 0) -> dict:
    arg_keys = jax.random.split(jax.random.key(seed), 8)
    return {
        "inputs": centred(arg_keys[0], (MICRO, TOKENS, D), 1.0, 6.0, ((1, 8),)),
        "route": draw_route(jax.random.fold_in(arg_keys[7], 71), 0),
        "gain": jnp.clip(1.0 + 0.18 * jax.random.normal(arg_keys[2], (LAYERS, D), jnp.float32), 0.099609375, 1.8984375).astype(jnp.bfloat16),
        "router": centred(arg_keys[3], (LAYERS, D, EXPERTS), D ** -0.5, 0.125, ((0, 4),)),
        "w_gate": centred(arg_keys[4], (LAYERS, EXPERTS, D, FF), D ** -0.5, 0.125, ((0, 4), (1, 8))),
        "w_up": centred(arg_keys[5], (LAYERS, EXPERTS, D, FF), D ** -0.5, 0.125, ((0, 4), (1, 8))),
        "w_down": centred(arg_keys[6], (LAYERS, EXPERTS, FF, D), FF ** -0.5, 0.21875, ((0, 4), (1, 8))),
    }


EPS = 1e-06

def expert_rows(rows, gate_mat, up_mat, down_mat):
    gate_act = jnp.dot(rows, gate_mat, preferred_element_type=jnp.float32)
    up_act = jnp.dot(rows, up_mat, preferred_element_type=jnp.float32)
    hidden = (jax.nn.silu(gate_act) * up_act).astype(jnp.bfloat16)
    return jnp.dot(hidden, down_mat, preferred_element_type=jnp.float32).astype(jnp.bfloat16)

def reference(inputs, route, gain, router, w_gate, w_up, w_down):
    row_limit = N_DP * CAP
    copy_total = TOKENS * TOP
    expert_ids = jnp.arange(EXPERTS, dtype=jnp.int32)
    layer_inputs = [inputs[micro_no] for micro_no in range(MICRO)]
    stacked = []
    for layer_no in range(LAYERS):
        outputs_now = []
        for micro_no in range(MICRO):
            layer_in = layer_inputs[micro_no]
            chosen_ids = route[layer_no, micro_no].astype(jnp.int32)
            wide_state = layer_in.astype(jnp.float32)
            inv_rms = lax.rsqrt(lax.optimization_barrier(jnp.mean(wide_state * wide_state, axis=1, keepdims=True)) + EPS)
            normed = (wide_state * inv_rms * gain[layer_no].astype(jnp.float32)).astype(jnp.bfloat16)
            logits = jnp.dot(normed, router[layer_no], preferred_element_type=jnp.float32)
            scores = jax.nn.sigmoid(jnp.take_along_axis(logits, chosen_ids, axis=1))
            weights = scores / lax.optimization_barrier(jnp.sum(scores, axis=1, keepdims=True))
            flat_ids = chosen_ids.reshape(-1)
            sorted_copies = jnp.argsort(flat_ids, stable=True).astype(jnp.int32)
            counts = lax.optimization_barrier(jnp.sum((flat_ids[:, None] == expert_ids[None, :]).astype(jnp.int32), axis=0))
            starts = (jnp.cumsum(counts) - counts).astype(jnp.int32)
            spot_list = starts[:, None] + jnp.arange(row_limit, dtype=jnp.int32)[None, :]
            keep_mask = jnp.arange(row_limit, dtype=jnp.int32)[None, :] < counts[:, None]
            copy_index = sorted_copies[jnp.clip(spot_list, 0, copy_total - 1)]

            def per_expert(expert_no):
                rows = normed[copy_index[expert_no] // TOP]
                return expert_rows(rows, w_gate[layer_no][expert_no], w_up[layer_no][expert_no], w_down[layer_no][expert_no])
            expert_out = lax.map(per_expert, expert_ids)
            target = jnp.where(keep_mask, copy_index, copy_total).reshape(-1)
            copies = jnp.zeros((copy_total + 1, D), jnp.bfloat16).at[target].set(expert_out.reshape(-1, D))[:copy_total]
            mixed = jnp.einsum('tk,tkd->td', weights, copies.reshape(TOKENS, TOP, D).astype(jnp.float32))
            outputs_now.append((wide_state + mixed).astype(jnp.bfloat16))
        layer_inputs = outputs_now
        stacked.append(jnp.stack(outputs_now))
    return jnp.stack(stacked)
```

```python
import functools

import jax
import jax.numpy as jnp
from jax import lax
from jax.experimental import pallas as pl
from jax.experimental.pallas import tpu as pltpu
from jax.sharding import PartitionSpec as P

EPS = 1e-06


def shifted(x, axis, by):
    devices = lax.axis_size(axis)
    pairs = [(i, i + by) for i in range(devices) if 0 <= i + by < devices]
    return lax.ppermute(x, axis, pairs)


def expert_rows(rows, gate_mat, up_mat, down_mat):
    gate_act = jnp.dot(rows, gate_mat, preferred_element_type=jnp.float32)
    up_act = jnp.dot(rows, up_mat, preferred_element_type=jnp.float32)
    hidden = (jax.nn.silu(gate_act) * up_act).astype(jnp.bfloat16)
    return jnp.dot(hidden, down_mat, preferred_element_type=jnp.float32).astype(jnp.bfloat16)


def on_device_sparse(inputs, route, gain, router, w_gate, w_up, w_down):
    section_count = lax.axis_size("section")
    section_index = lax.axis_index("section")
    micro_count, tok_rows, model_width = inputs.shape
    top_count = route.shape[-1]
    experts = router.shape[-1]
    pair_load = 2 * tok_rows * top_count // experts
    capacity = min(pair_load, tok_rows)
    slot_count = experts * capacity
    gate_mat = w_gate[0, 0]
    up_mat = w_up[0, 0]
    down_mat = w_down[0, 0]
    gain_row = gain[0].astype(jnp.float32)
    router_mat = router[0]
    expert_ids = jnp.arange(experts, dtype=jnp.int32)
    slot_ids = jnp.arange(slot_count, dtype=jnp.int32)

    def compute_all(flat_rows):
        return expert_rows(flat_rows, gate_mat, up_mat, down_mat)

    def skip_all(flat_rows):
        return jnp.zeros_like(flat_rows)

    inbound = jnp.zeros((tok_rows, model_width), jnp.bfloat16)
    states = jnp.zeros((micro_count, tok_rows, model_width), jnp.bfloat16)
    for tick_no in range(micro_count + section_count - 1):
        micro_now = tick_no - section_index
        active = (micro_now >= 0) & (micro_now < micro_count)
        micro_index = jnp.clip(micro_now, 0, micro_count - 1)
        fresh_rows = lax.dynamic_index_in_dim(inputs, micro_index, 0, keepdims=False)
        current = jnp.where(section_index == 0, fresh_rows, inbound)
        chosen_ids = lax.dynamic_index_in_dim(route[0], micro_index, 0, keepdims=False)
        wide_state = current.astype(jnp.float32)
        inv_rms = lax.rsqrt(jnp.mean(wide_state * wide_state, axis=1, keepdims=True) + EPS)
        normed = (wide_state * inv_rms * gain_row).astype(jnp.bfloat16)
        logits = jnp.dot(normed, router_mat, preferred_element_type=jnp.float32)
        scores = jax.nn.sigmoid(jnp.take_along_axis(logits, chosen_ids, axis=1))
        weights = scores / jnp.sum(scores, axis=1, keepdims=True)
        flat_ids = chosen_ids.reshape(-1)
        onehot = (flat_ids[:, None] == expert_ids[None, :]).astype(jnp.int32)
        slot_rank = jnp.sum((jnp.cumsum(onehot, axis=0) - onehot) * onehot, axis=1)
        target = flat_ids * capacity + slot_rank
        selector = (target[None, :] == slot_ids[:, None]) & active
        by_token = jnp.sum(
            selector.reshape(slot_count, tok_rows, top_count).astype(jnp.int32), axis=2
        )
        buffer = jnp.dot(
            by_token.astype(jnp.bfloat16), normed, preferred_element_type=jnp.float32
        ).astype(jnp.bfloat16)
        live_slots = jnp.sum(by_token, axis=1).reshape(experts, capacity)
        slot_buffer = buffer.reshape(experts, capacity, model_width)
        slot_rows = lax.all_to_all(slot_buffer, "dp", split_axis=0, concat_axis=0, tiled=True)
        slot_live = lax.all_to_all(live_slots, "dp", split_axis=0, concat_axis=0, tiled=True)
        source_count, item_count = slot_live.shape
        row_count = source_count * item_count
        run_flat_rows = slot_rows.reshape(row_count, model_width)
        live_flat = slot_live.reshape(row_count)
        expert_out = lax.cond(jnp.any(live_flat > 0), compute_all, skip_all, run_flat_rows)
        expert_out = expert_out.reshape(source_count, item_count, model_width)
        returned = lax.all_to_all(expert_out, "dp", split_axis=0, concat_axis=0, tiled=True)
        copies = returned.reshape(slot_count, model_width)[target].reshape(
            tok_rows, top_count, model_width
        )
        mixed = jnp.einsum("tk,tkd->td", weights, copies.astype(jnp.float32))
        layer_out = (wide_state + mixed).astype(jnp.bfloat16)
        previous = lax.dynamic_index_in_dim(states, micro_index, 0, keepdims=False)
        states = lax.dynamic_update_index_in_dim(
            states, jnp.where(active, layer_out, previous), micro_index, 0
        )
        inbound = shifted(layer_out, "section", 1)
    return states[None]


HALF = 64
LANES = 2 * HALF
MESH = pl.DeviceIdType.MESH


def relay_kernel(
    sections, line, chunks, rows,
    x_ref, route_ref, gain_ref, router_ref, gate_hbm, up_hbm, down_hbm, out_ref,
    gate_v, up_v, down_v, state, gathered, part, peer_part, relay, hidden, total,
    w_sem, x_send, x_recv, ag_send, ag_recv, ex_send, ex_recv, rs_send, rs_recv,
):
    sec = lax.axis_index("section")
    dpi = lax.axis_index("dp")
    z = dpi // 2
    core = dpi % 2
    width = x_ref.shape[1]
    ff = gate_v.shape[1]
    last = line - 1
    has_left, has_right = z > 0, z < last

    partner = (sec, z * 2 + 1 - core)
    right = (sec, jnp.minimum(dpi + 2, 2 * line - 1))
    left = (sec, jnp.maximum(dpi - 2, 0))
    after = (jnp.minimum(sec + 1, sections - 1), dpi)
    before = (jnp.maximum(sec - 1, 0), dpi)

    def span(j):
        return pl.ds(pl.multiple_of(j * rows, rows), rows)

    def ag_copy(kind, j, src):
        block = gathered.at[j, core, src]
        return pltpu.make_async_remote_copy(
            block, block, ag_send.at[j, kind, src], ag_recv.at[j, core, src],
            device_id=(right, left, partner)[kind], device_id_type=MESH,
        )

    def ag_arrival(j, which, src):
        block = gathered.at[j, which, src]
        pltpu.make_async_remote_copy(
            block, block, ag_send.at[j, 0, src], ag_recv.at[j, which, src],
            device_id=partner, device_id_type=MESH,
        ).wait_recv()

    def ex_copy(j):
        return pltpu.make_async_remote_copy(
            part.at[j, 1 - core], peer_part.at[j], ex_send.at[j], ex_recv.at[j],
            device_id=partner, device_id_type=MESH,
        )

    def rs_copy(way, j, dest):
        block = relay.at[j, way, dest]
        return pltpu.make_async_remote_copy(
            block, block, rs_send.at[j, way, dest], rs_recv.at[j, way, dest],
            device_id=(right, left)[way], device_id_type=MESH,
        )

    def x_copy(j):
        return pltpu.make_async_remote_copy(
            out_ref.at[span(j)], state.at[j], x_send.at[j], x_recv.at[j],
            device_id=after, device_id_type=MESH,
        )

    weight_copies = [
        pltpu.make_async_copy(gate_hbm, gate_v, w_sem.at[0]),
        pltpu.make_async_copy(up_hbm, up_v, w_sem.at[1]),
        pltpu.make_async_copy(down_hbm, down_v, w_sem.at[2]),
    ]
    for copy in weight_copies:
        copy.start()

    barrier = pltpu.get_barrier_semaphore()
    neighbours = (
        (None, partner),
        (has_left, left),
        (has_right, right),
        (sec > 0, before),
        (sec < sections - 1, after),
    )
    for cond, device in neighbours:
        def greet(device=device):
            pl.semaphore_signal(barrier, inc=1, device_id=device, device_id_type=MESH)
        if cond is None:
            greet()
        else:
            pl.when(cond)(greet)
    peers = 1
    for cond, _ in neighbours[1:]:
        peers += jnp.where(cond, 1, 0)
    pl.semaphore_wait(barrier, peers)

    def enter(j):
        @pl.when(sec == 0)
        def _():
            state[j] = x_ref[span(j)]

        @pl.when(sec > 0)
        def _():
            x_copy(j).wait_recv()

        wide = state[j].astype(jnp.float32)
        inv_rms = lax.rsqrt(jnp.mean(wide * wide, axis=1, keepdims=True) + EPS)
        normed = (wide * inv_rms * gain_ref[...].astype(jnp.float32)).astype(jnp.bfloat16)
        logits = jnp.dot(normed, router_ref[...], preferred_element_type=jnp.float32)
        lane = lax.broadcasted_iota(jnp.int32, (rows, LANES), 1)
        folded = jnp.where(lane < HALF, lane, lane - HALF)
        chosen = route_ref[span(j)]
        named = folded == chosen[:, 0:1]
        for k in range(1, chosen.shape[1]):
            named = named | (folded == chosen[:, k:k + 1])
        scores = jnp.where(named, jax.nn.sigmoid(logits), 0.0)
        norm = jnp.sum(jnp.where(lane < HALF, scores, 0.0), axis=1, keepdims=True)
        weights = scores / norm
        high = weights.astype(jnp.bfloat16).astype(jnp.float32)
        carried = jnp.where(lane < HALF, high, weights - high)
        gathered[j, core, z, :, 0:width] = normed
        gathered[j, core, z, :, width:width + LANES] = carried.astype(jnp.bfloat16)

        @pl.when(has_right)
        def _():
            ag_copy(0, j, z).start()

        @pl.when(has_left)
        def _():
            ag_copy(1, j, z).start()

        ag_copy(2, j, z).start()

    def gather_hop(hop, j):
        @pl.when(z >= hop)
        def _():
            ag_arrival(j, core, z - hop)

            @pl.when(has_right)
            def _():
                ag_copy(0, j, z - hop).start()

            ag_copy(2, j, z - hop).start()

        @pl.when(z + hop <= last)
        def _():
            ag_arrival(j, core, z + hop)

            @pl.when(has_left)
            def _():
                ag_copy(1, j, z + hop).start()

            ag_copy(2, j, z + hop).start()

    def compute(j):
        for src in range(line):
            ag_arrival(j, 1 - core, src)
        count = 2 * line * rows
        block = gathered[j, :, :, :, 0:width].reshape(count, width)
        carried = gathered[j, :, :, :, width:width + LANES].reshape(count, LANES).astype(jnp.float32)
        lane = lax.broadcasted_iota(jnp.int32, (count, LANES), 1)
        mine = (lane == dpi) | (lane == dpi + HALF)
        weight = jnp.sum(jnp.where(mine, carried, 0.0), axis=1, keepdims=True)
        step = 256
        for lo in range(0, ff, step):
            cols = slice(lo, lo + step)
            gate = jnp.dot(block, gate_v[:, cols], preferred_element_type=jnp.float32)
            up = jnp.dot(block, up_v[:, cols], preferred_element_type=jnp.float32)
            hidden[:, cols] = (jax.nn.silu(gate) * up * weight).astype(jnp.bfloat16)
        for lo in range(0, width, 2 * step):
            cols = slice(lo, lo + 2 * step)
            done = jnp.dot(hidden[...], down_v[:, cols], preferred_element_type=jnp.float32)
            part[j, :, :, :, cols] = done.astype(jnp.bfloat16).reshape(2, line, rows, 2 * step)
        ex_copy(j).start()

    def pair_sum(j, dest):
        return part[j, core, dest].astype(jnp.float32) + peer_part[j, dest].astype(jnp.float32)

    def reduce_hop(hop, j):
        for way in range(2):
            place = z if way == 0 else last - z
            dest = z + line - hop if way == 0 else z - line + hop

            @pl.when(place <= hop - 1)
            def _():
                @pl.when(place == 0)
                def _():
                    relay[j, way, dest] = pair_sum(j, dest).astype(jnp.bfloat16)

                @pl.when(place > 0)
                def _():
                    rs_copy(way, j, dest).wait_recv()
                    held = relay[j, way, dest].astype(jnp.float32)
                    relay[j, way, dest] = (pair_sum(j, dest) + held).astype(jnp.bfloat16)

                rs_copy(way, j, dest).start()

    def leave(j):
        total[...] = state[j].astype(jnp.float32) + pair_sum(j, z)

        @pl.when(has_left)
        def _():
            rs_copy(0, j, z).wait_recv()
            total[...] += relay[j, 0, z].astype(jnp.float32)

        @pl.when(has_right)
        def _():
            rs_copy(1, j, z).wait_recv()
            total[...] += relay[j, 1, z].astype(jnp.float32)

        out_ref[span(j)] = total[...].astype(jnp.bfloat16)

        @pl.when(sec < sections - 1)
        def _():
            x_copy(j).start()

    def settle(j):
        for src in range(line):
            @pl.when(has_right & (src <= z))
            def _():
                ag_copy(0, j, src).wait_send()

            @pl.when(has_left & (src >= z))
            def _():
                ag_copy(1, j, src).wait_send()

            ag_copy(2, j, src).wait_send()

            @pl.when(has_right & (src > z))
            def _():
                rs_copy(0, j, src).wait_send()

            @pl.when(has_left & (src < z))
            def _():
                rs_copy(1, j, src).wait_send()

        ex_copy(j).wait_send()

        @pl.when(sec < sections - 1)
        def _():
            x_copy(j).wait_send()

    depth = 2 * line - 1

    def round_step(r, carry):
        def phase(late, work):
            j = r - late

            @pl.when((j >= 0) & (j < chunks))
            def _():
                work(j)

        phase(depth, leave)
        for hop in range(last, 0, -1):
            def work(j, hop=hop):
                if hop == 1:
                    ex_copy(j).wait_recv()
                reduce_hop(hop, j)
            phase(last + hop, work)
        for hop in range(last, 0, -1):
            phase(hop, functools.partial(gather_hop, hop))

        @pl.when(r == last)
        def _():
            for copy in weight_copies:
                copy.wait()

        phase(last, compute)
        phase(0, enter)
        return carry

    lax.fori_loop(0, chunks + depth, round_step, 0)

    def settle_step(j, carry):
        settle(j)
        return carry

    lax.fori_loop(0, chunks, settle_step, 0)


def on_device_dense(shape, inputs, route, gain, router, w_gate, w_up, w_down):
    sections = shape["section"]
    line = shape["dp"] // 2
    micro_count, tok_rows, width = inputs.shape
    top = route.shape[-1]
    experts = router.shape[-1]
    ff = w_gate.shape[-1]
    rows = min(ROWS, tok_rows)
    token_rows = micro_count * tok_rows
    chunks = token_rows // rows
    padded = jnp.pad(router[0], ((0, 0), (0, HALF - experts)))
    router_mat = jnp.concatenate([padded, padded], axis=1)
    bf16 = jnp.bfloat16
    count = 2 * line * rows
    dma = pltpu.SemaphoreType.DMA
    vmem = pl.BlockSpec(memory_space=pltpu.VMEM)
    far = pl.BlockSpec(memory_space=pl.ANY)
    flops = 6 * chunks * count * width * ff
    result = pl.pallas_call(
        functools.partial(relay_kernel, sections, line, chunks, rows),
        out_shape=jax.ShapeDtypeStruct((token_rows, width), bf16),
        in_specs=[vmem] * 4 + [far] * 3,
        out_specs=vmem,
        scratch_shapes=[
            pltpu.VMEM((width, ff), bf16),
            pltpu.VMEM((width, ff), bf16),
            pltpu.VMEM((ff, width), bf16),
            pltpu.VMEM((chunks, rows, width), bf16),
            pltpu.VMEM((chunks, 2, line, rows, width + LANES), bf16),
            pltpu.VMEM((chunks, 2, line, rows, width), bf16),
            pltpu.VMEM((chunks, line, rows, width), bf16),
            pltpu.VMEM((chunks, 2, line, rows, width), bf16),
            pltpu.VMEM((count, ff), bf16),
            pltpu.VMEM((rows, width), jnp.float32),
            dma((3,)),
            dma((chunks,)),
            dma((chunks,)),
            dma((chunks, 3, line)),
            dma((chunks, 2, line)),
            dma((chunks,)),
            dma((chunks,)),
            dma((chunks, 2, line)),
            dma((chunks, 2, line)),
        ],
        compiler_params=pltpu.CompilerParams(
            collective_id=0, has_side_effects=True, vmem_limit_bytes=56 * 2**20
        ),
        cost_estimate=pl.CostEstimate(
            flops=flops, bytes_accessed=6 * width * ff, transcendentals=chunks * count * ff
        ),
    )(
        inputs.reshape(token_rows, width),
        route.reshape(token_rows, top),
        gain,
        router_mat,
        w_gate[0, 0],
        w_up[0, 0],
        w_down[0, 0],
    )
    return result.reshape(1, micro_count, tok_rows, width)


ROWS = 16


def on_device(shape, inputs, route, gain, router, w_gate, w_up, w_down):
    tok_rows = inputs.shape[1]
    experts = router.shape[-1]
    args = (inputs, route, gain, router, w_gate, w_up, w_down)
    if 2 * tok_rows * route.shape[-1] // experts >= tok_rows and experts <= HALF:
        return on_device_dense(shape, *args)
    return on_device_sparse(*args)


def solution(mesh):
    body = functools.partial(on_device, dict(mesh.shape))
    in_specs = (
        P(None, "dp", None),
        P("section", None, "dp", None),
        P("section", None),
        P("section", None, None),
        P("section", "dp", None, None),
        P("section", "dp", None, None),
        P("section", "dp", None, None),
    )
    out_specs = P("section", None, "dp", None)
    return jax.shard_map(
        body, mesh=mesh, in_specs=in_specs, out_specs=out_specs, check_vma=False
    )
```

```python
import functools

import jax
import jax.numpy as jnp
from jax import lax
from jax.experimental import pallas as pl
from jax.experimental.pallas import tpu as pltpu
from jax.sharding import PartitionSpec as P

EPS = 1e-06


def shifted(x, axis, by):
    devices = lax.axis_size(axis)
    pairs = [(i, i + by) for i in range(devices) if 0 <= i + by < devices]
    return lax.ppermute(x, axis, pairs)


def expert_rows(rows, gate_mat, up_mat, down_mat):
    gate_act = jnp.dot(rows, gate_mat, preferred_element_type=jnp.float32)
    up_act = jnp.dot(rows, up_mat, preferred_element_type=jnp.float32)
    hidden = (jax.nn.silu(gate_act) * up_act).astype(jnp.bfloat16)
    return jnp.dot(hidden, down_mat, preferred_element_type=jnp.float32).astype(jnp.bfloat16)


def on_device_sparse(inputs, route, gain, router, w_gate, w_up, w_down):
    section_count = lax.axis_size("section")
    section_index = lax.axis_index("section")
    micro_count, tok_rows, model_width = inputs.shape
    top_count = route.shape[-1]
    experts = router.shape[-1]
    pair_load = 2 * tok_rows * top_count // experts
    capacity = min(pair_load, tok_rows)
    slot_count = experts * capacity
    gate_mat = w_gate[0, 0]
    up_mat = w_up[0, 0]
    down_mat = w_down[0, 0]
    gain_row = gain[0].astype(jnp.float32)
    router_mat = router[0]
    expert_ids = jnp.arange(experts, dtype=jnp.int32)
    slot_ids = jnp.arange(slot_count, dtype=jnp.int32)

    def compute_all(flat_rows):
        return expert_rows(flat_rows, gate_mat, up_mat, down_mat)

    def skip_all(flat_rows):
        return jnp.zeros_like(flat_rows)

    inbound = jnp.zeros((tok_rows, model_width), jnp.bfloat16)
    states = jnp.zeros((micro_count, tok_rows, model_width), jnp.bfloat16)
    for tick_no in range(micro_count + section_count - 1):
        micro_now = tick_no - section_index
        active = (micro_now >= 0) & (micro_now < micro_count)
        micro_index = jnp.clip(micro_now, 0, micro_count - 1)
        fresh_rows = lax.dynamic_index_in_dim(inputs, micro_index, 0, keepdims=False)
        current = jnp.where(section_index == 0, fresh_rows, inbound)
        chosen_ids = lax.dynamic_index_in_dim(route[0], micro_index, 0, keepdims=False)
        wide_state = current.astype(jnp.float32)
        inv_rms = lax.rsqrt(jnp.mean(wide_state * wide_state, axis=1, keepdims=True) + EPS)
        normed = (wide_state * inv_rms * gain_row).astype(jnp.bfloat16)
        logits = jnp.dot(normed, router_mat, preferred_element_type=jnp.float32)
        scores = jax.nn.sigmoid(jnp.take_along_axis(logits, chosen_ids, axis=1))
        weights = scores / jnp.sum(scores, axis=1, keepdims=True)
        flat_ids = chosen_ids.reshape(-1)
        onehot = (flat_ids[:, None] == expert_ids[None, :]).astype(jnp.int32)
        slot_rank = jnp.sum((jnp.cumsum(onehot, axis=0) - onehot) * onehot, axis=1)
        target = flat_ids * capacity + slot_rank
        selector = (target[None, :] == slot_ids[:, None]) & active
        by_token = jnp.sum(
            selector.reshape(slot_count, tok_rows, top_count).astype(jnp.int32), axis=2
        )
        buffer = jnp.dot(
            by_token.astype(jnp.bfloat16), normed, preferred_element_type=jnp.float32
        ).astype(jnp.bfloat16)
        live_slots = jnp.sum(by_token, axis=1).reshape(experts, capacity)
        slot_buffer = buffer.reshape(experts, capacity, model_width)
        slot_rows = lax.all_to_all(slot_buffer, "dp", split_axis=0, concat_axis=0, tiled=True)
        slot_live = lax.all_to_all(live_slots, "dp", split_axis=0, concat_axis=0, tiled=True)
        source_count, item_count = slot_live.shape
        row_count = source_count * item_count
        run_flat_rows = slot_rows.reshape(row_count, model_width)
        live_flat = slot_live.reshape(row_count)
        expert_out = lax.cond(jnp.any(live_flat > 0), compute_all, skip_all, run_flat_rows)
        expert_out = expert_out.reshape(source_count, item_count, model_width)
        returned = lax.all_to_all(expert_out, "dp", split_axis=0, concat_axis=0, tiled=True)
        copies = returned.reshape(slot_count, model_width)[target].reshape(
            tok_rows, top_count, model_width
        )
        mixed = jnp.einsum("tk,tkd->td", weights, copies.astype(jnp.float32))
        layer_out = (wide_state + mixed).astype(jnp.bfloat16)
        previous = lax.dynamic_index_in_dim(states, micro_index, 0, keepdims=False)
        states = lax.dynamic_update_index_in_dim(
            states, jnp.where(active, layer_out, previous), micro_index, 0
        )
        inbound = shifted(layer_out, "section", 1)
    return states[None]


HALF = 64
LANES = 2 * HALF
SLICE = 512
MESH = pl.DeviceIdType.MESH


def relay_kernel(
    sections, line, chunks, rows,
    x_ref, route_ref, gain_ref, router_ref, gate_hbm, up_hbm, down_hbm, out_ref,
    gate_v, up_v, down_v, state, gathered, part, peer_part, stage, near_in, far_in, hidden,
    w_sem, x_send, x_recv, mate_send, cross_send, pair_send, ag_recv, ex_send, ex_recv,
    near_send, near_recv, far_send, far_recv,
):
    sec = lax.axis_index("section")
    dpi = lax.axis_index("dp")
    z = dpi // 2
    core = dpi % 2
    width = x_ref.shape[1]
    ff = gate_v.shape[1]
    low_half = z < 2
    inner = (z == 1) | (z == 2)
    mate_z = z + 1 - 2 * (z % 2)
    cross_z = jnp.where(low_half, 2, 1)
    edge_z = jnp.where(low_half, 3, 0)

    partner = (sec, z * 2 + 1 - core)
    mate = (sec, mate_z * 2 + core)
    cross = (sec, cross_z * 2 + core)
    edge = (sec, edge_z * 2 + core)
    after = (jnp.minimum(sec + 1, sections - 1), dpi)
    before = (jnp.maximum(sec - 1, 0), dpi)

    def span(j):
        return pl.ds(pl.multiple_of(j * rows, rows), rows)

    def remote(src, dst, send, recv, device):
        return pltpu.make_async_remote_copy(
            src, dst, send, recv, device_id=device, device_id_type=MESH
        )

    def to_mate(j, src):
        block = gathered.at[j, core, src]
        return remote(block, block, mate_send.at[j, src], ag_recv.at[j, core, src], mate)

    def to_cross(j):
        block = gathered.at[j, core, z]
        return remote(block, block, cross_send.at[j], ag_recv.at[j, core, z], cross)

    def to_partner(j, src):
        block = gathered.at[j, core, src]
        return remote(block, block, pair_send.at[j, src], ag_recv.at[j, core, src], partner)

    def ag_arrival(j, which, src):
        block = gathered.at[j, which, src]
        remote(block, block, pair_send.at[j, src], ag_recv.at[j, which, src], partner).wait_recv()

    def ex_copy(j, piece):
        cols = pl.ds(piece * SLICE, SLICE)
        return remote(
            part.at[j, 1 - core, :, :, cols], peer_part.at[j, :, :, cols],
            ex_send.at[j, piece], ex_recv.at[j, piece], partner,
        )

    def near_copy(j, dest):
        return remote(
            stage.at[j, dest], near_in.at[j, dest], near_send.at[j, dest], near_recv.at[j, dest], mate
        )

    def far_copy(j, which):
        dest, device = ((cross_z, cross), (edge_z, edge))[which]
        return remote(stage.at[j, dest], far_in.at[j], far_send.at[j, which], far_recv.at[j], device)

    def x_copy(j):
        return pltpu.make_async_remote_copy(
            out_ref.at[span(j)], state.at[j], x_send.at[j], x_recv.at[j],
            device_id=after, device_id_type=MESH,
        )

    weight_copies = [
        pltpu.make_async_copy(gate_hbm, gate_v, w_sem.at[0]),
        pltpu.make_async_copy(up_hbm, up_v, w_sem.at[1]),
        pltpu.make_async_copy(down_hbm, down_v, w_sem.at[2]),
    ]
    for copy in weight_copies:
        copy.start()

    barrier = pltpu.get_barrier_semaphore()
    neighbours = (
        (None, partner),
        (None, mate),
        (None, cross),
        (inner, edge),
        (sec > 0, before),
        (sec < sections - 1, after),
    )
    for cond, device in neighbours:
        def greet(device=device):
            pl.semaphore_signal(barrier, inc=1, device_id=device, device_id_type=MESH)
        if cond is None:
            greet()
        else:
            pl.when(cond)(greet)
    peers = 3
    for cond, _ in neighbours[3:]:
        peers += jnp.where(cond, 1, 0)
    pl.semaphore_wait(barrier, peers)

    def enter(j):
        @pl.when(sec == 0)
        def _():
            state[j] = x_ref[span(j)]

        @pl.when(sec > 0)
        def _():
            x_copy(j).wait_recv()

        wide = state[j].astype(jnp.float32)
        inv_rms = lax.rsqrt(jnp.mean(wide * wide, axis=1, keepdims=True) + EPS)
        normed = (wide * inv_rms * gain_ref[...].astype(jnp.float32)).astype(jnp.bfloat16)
        logits = jnp.dot(normed, router_ref[...], preferred_element_type=jnp.float32)
        lane = lax.broadcasted_iota(jnp.int32, (rows, LANES), 1)
        folded = jnp.where(lane < HALF, lane, lane - HALF)
        chosen = route_ref[span(j)]
        named = folded == chosen[:, 0:1]
        for k in range(1, chosen.shape[1]):
            named = named | (folded == chosen[:, k:k + 1])
        scores = jnp.where(named, jax.nn.sigmoid(logits), 0.0)
        norm = jnp.sum(jnp.where(lane < HALF, scores, 0.0), axis=1, keepdims=True)
        weights = scores / norm
        high = weights.astype(jnp.bfloat16).astype(jnp.float32)
        carried = jnp.where(lane < HALF, high, weights - high)
        gathered[j, core, z, :, 0:width] = normed
        gathered[j, core, z, :, width:width + LANES] = carried.astype(jnp.bfloat16)

        to_cross(j).start()
        to_mate(j, z).start()
        to_partner(j, z).start()

    def gather_near(j):
        @pl.when(inner)
        def _():
            for src in (cross_z, edge_z):
                ag_arrival(j, core, src)
                to_mate(j, src).start()
                to_partner(j, src).start()

        ag_arrival(j, core, mate_z)
        to_partner(j, mate_z).start()

    def gather_far(j):
        @pl.when(jnp.logical_not(inner))
        def _():
            for src in (cross_z, edge_z):
                ag_arrival(j, core, src)
                to_partner(j, src).start()

    def compute(j):
        for src in range(line):
            ag_arrival(j, 1 - core, src)
        count = 2 * line * rows
        block = gathered[j, :, :, :, 0:width].reshape(count, width)
        carried = gathered[j, :, :, :, width:width + LANES].reshape(count, LANES).astype(jnp.float32)
        lane = lax.broadcasted_iota(jnp.int32, (count, LANES), 1)
        mine = (lane == dpi) | (lane == dpi + HALF)
        weight = jnp.sum(jnp.where(mine, carried, 0.0), axis=1, keepdims=True)
        step = 256
        for lo in range(0, ff, step):
            cols = slice(lo, lo + step)
            gate = jnp.dot(block, gate_v[:, cols], preferred_element_type=jnp.float32)
            up = jnp.dot(block, up_v[:, cols], preferred_element_type=jnp.float32)
            hidden[:, cols] = (jax.nn.silu(gate) * up * weight).astype(jnp.bfloat16)
        for piece in range(width // SLICE):
            cols = slice(piece * SLICE, piece * SLICE + SLICE)
            done = jnp.dot(hidden[...], down_v[:, cols], preferred_element_type=jnp.float32)
            part[j, :, :, :, cols] = done.astype(jnp.bfloat16).reshape(2, line, rows, SLICE)
            ex_copy(j, piece).start()

    def pair_sum(j, dest):
        return part[j, core, dest].astype(jnp.float32) + peer_part[j, dest].astype(jnp.float32)

    def reduce_near(j):
        for piece in range(width // SLICE):
            ex_copy(j, piece).wait_recv()

        @pl.when(jnp.logical_not(inner))
        def _():
            for dest in (edge_z, cross_z):
                stage[j, dest] = pair_sum(j, dest).astype(jnp.bfloat16)
                near_copy(j, dest).start()

        stage[j, mate_z] = pair_sum(j, mate_z).astype(jnp.bfloat16)
        near_copy(j, mate_z).start()

    def reduce_far(j):
        @pl.when(inner)
        def _():
            for which, dest in ((1, edge_z), (0, cross_z)):
                near_copy(j, dest).wait_recv()
                held = near_in[j, dest].astype(jnp.float32)
                stage[j, dest] = (pair_sum(j, dest) + held).astype(jnp.bfloat16)
                far_copy(j, which).start()

    def leave(j):
        near_copy(j, z).wait_recv()
        far_copy(j, 0).wait_recv()
        held = near_in[j, z].astype(jnp.float32) + far_in[j].astype(jnp.float32)
        total = state[j].astype(jnp.float32) + (pair_sum(j, z) + held)
        out_ref[span(j)] = total.astype(jnp.bfloat16)

        @pl.when(sec < sections - 1)
        def _():
            x_copy(j).start()

    def settle(j):
        to_cross(j).wait_send()
        to_mate(j, z).wait_send()
        for src in range(line):
            to_partner(j, src).wait_send()
        for piece in range(width // SLICE):
            ex_copy(j, piece).wait_send()
        near_copy(j, mate_z).wait_send()

        @pl.when(inner)
        def _():
            for which, src in ((1, edge_z), (0, cross_z)):
                to_mate(j, src).wait_send()
                far_copy(j, which).wait_send()

        @pl.when(jnp.logical_not(inner))
        def _():
            for dest in (edge_z, cross_z):
                near_copy(j, dest).wait_send()

        @pl.when(sec < sections - 1)
        def _():
            x_copy(j).wait_send()

    depth = 5

    def round_step(r, carry):
        def phase(late, work):
            j = r - late

            @pl.when((j >= 0) & (j < chunks))
            def _():
                work(j)

        phase(2, gather_far)
        phase(1, gather_near)
        phase(5, leave)
        phase(4, reduce_far)
        phase(3, reduce_near)
        phase(0, enter)

        @pl.when(r == 2)
        def _():
            for copy in weight_copies:
                copy.wait()

        phase(2, compute)
        return carry

    lax.fori_loop(0, chunks + depth, round_step, 0)

    def settle_step(j, carry):
        settle(j)
        return carry

    lax.fori_loop(0, chunks, settle_step, 0)


def on_device_dense(shape, inputs, route, gain, router, w_gate, w_up, w_down):
    sections = shape["section"]
    line = shape["dp"] // 2
    micro_count, tok_rows, width = inputs.shape
    top = route.shape[-1]
    experts = router.shape[-1]
    ff = w_gate.shape[-1]
    rows = min(ROWS, tok_rows)
    token_rows = micro_count * tok_rows
    chunks = token_rows // rows
    padded = jnp.pad(router[0], ((0, 0), (0, HALF - experts)))
    router_mat = jnp.concatenate([padded, padded], axis=1)
    bf16 = jnp.bfloat16
    count = 2 * line * rows
    dma = pltpu.SemaphoreType.DMA
    vmem = pl.BlockSpec(memory_space=pltpu.VMEM)
    far = pl.BlockSpec(memory_space=pl.ANY)
    flops = 6 * chunks * count * width * ff
    result = pl.pallas_call(
        functools.partial(relay_kernel, sections, line, chunks, rows),
        out_shape=jax.ShapeDtypeStruct((token_rows, width), bf16),
        in_specs=[vmem] * 4 + [far] * 3,
        out_specs=vmem,
        scratch_shapes=[
            pltpu.VMEM((width, ff), bf16),
            pltpu.VMEM((width, ff), bf16),
            pltpu.VMEM((ff, width), bf16),
            pltpu.VMEM((chunks, rows, width), bf16),
            pltpu.VMEM((chunks, 2, line, rows, width + LANES), bf16),
            pltpu.VMEM((chunks, 2, line, rows, width), bf16),
            pltpu.VMEM((chunks, line, rows, width), bf16),
            pltpu.VMEM((chunks, line, rows, width), bf16),
            pltpu.VMEM((chunks, line, rows, width), bf16),
            pltpu.VMEM((chunks, rows, width), bf16),
            pltpu.VMEM((count, ff), bf16),
            dma((3,)),
            dma((chunks,)),
            dma((chunks,)),
            dma((chunks, line)),
            dma((chunks,)),
            dma((chunks, line)),
            dma((chunks, 2, line)),
            dma((chunks, width // SLICE)),
            dma((chunks, width // SLICE)),
            dma((chunks, line)),
            dma((chunks, line)),
            dma((chunks, 2)),
            dma((chunks,)),
        ],
        compiler_params=pltpu.CompilerParams(
            collective_id=0, has_side_effects=True, vmem_limit_bytes=56 * 2**20
        ),
        cost_estimate=pl.CostEstimate(
            flops=flops, bytes_accessed=6 * width * ff, transcendentals=chunks * count * ff
        ),
    )(
        inputs.reshape(token_rows, width),
        route.reshape(token_rows, top),
        gain,
        router_mat,
        w_gate[0, 0],
        w_up[0, 0],
        w_down[0, 0],
    )
    return result.reshape(1, micro_count, tok_rows, width)


ROWS = 16


def on_device(shape, inputs, route, gain, router, w_gate, w_up, w_down):
    tok_rows = inputs.shape[1]
    experts = router.shape[-1]
    args = (inputs, route, gain, router, w_gate, w_up, w_down)
    if 2 * tok_rows * route.shape[-1] // experts >= tok_rows and experts <= HALF and shape["dp"] == 8:
        return on_device_dense(shape, *args)
    return on_device_sparse(*args)


def solution(mesh):
    body = functools.partial(on_device, dict(mesh.shape))
    in_specs = (
        P(None, "dp", None),
        P("section", None, "dp", None),
        P("section", None),
        P("section", None, None),
        P("section", "dp", None, None),
        P("section", "dp", None, None),
        P("section", "dp", None, None),
    )
    out_specs = P("section", None, "dp", None)
    return jax.shard_map(
        body, mesh=mesh, in_specs=in_specs, out_specs=out_specs, check_vma=False
    )
```

```python
import functools

import jax
import jax.numpy as jnp
from jax import lax
from jax.experimental import pallas as pl
from jax.experimental.pallas import tpu as pltpu
from jax.sharding import PartitionSpec as P

EPS = 1e-06


def shifted(x, axis, by):
    devices = lax.axis_size(axis)
    pairs = [(i, i + by) for i in range(devices) if 0 <= i + by < devices]
    return lax.ppermute(x, axis, pairs)


def expert_rows(rows, gate_mat, up_mat, down_mat):
    gate_act = jnp.dot(rows, gate_mat, preferred_element_type=jnp.float32)
    up_act = jnp.dot(rows, up_mat, preferred_element_type=jnp.float32)
    hidden = (jax.nn.silu(gate_act) * up_act).astype(jnp.bfloat16)
    return jnp.dot(hidden, down_mat, preferred_element_type=jnp.float32).astype(jnp.bfloat16)


def on_device_sparse(inputs, route, gain, router, w_gate, w_up, w_down):
    section_count = lax.axis_size("section")
    section_index = lax.axis_index("section")
    micro_count, tok_rows, model_width = inputs.shape
    top_count = route.shape[-1]
    experts = router.shape[-1]
    pair_load = 2 * tok_rows * top_count // experts
    capacity = min(pair_load, tok_rows)
    slot_count = experts * capacity
    gate_mat = w_gate[0, 0]
    up_mat = w_up[0, 0]
    down_mat = w_down[0, 0]
    gain_row = gain[0].astype(jnp.float32)
    router_mat = router[0]
    expert_ids = jnp.arange(experts, dtype=jnp.int32)
    slot_ids = jnp.arange(slot_count, dtype=jnp.int32)

    def compute_all(flat_rows):
        return expert_rows(flat_rows, gate_mat, up_mat, down_mat)

    def skip_all(flat_rows):
        return jnp.zeros_like(flat_rows)

    inbound = jnp.zeros((tok_rows, model_width), jnp.bfloat16)
    states = jnp.zeros((micro_count, tok_rows, model_width), jnp.bfloat16)
    for tick_no in range(micro_count + section_count - 1):
        micro_now = tick_no - section_index
        active = (micro_now >= 0) & (micro_now < micro_count)
        micro_index = jnp.clip(micro_now, 0, micro_count - 1)
        fresh_rows = lax.dynamic_index_in_dim(inputs, micro_index, 0, keepdims=False)
        current = jnp.where(section_index == 0, fresh_rows, inbound)
        chosen_ids = lax.dynamic_index_in_dim(route[0], micro_index, 0, keepdims=False)
        wide_state = current.astype(jnp.float32)
        inv_rms = lax.rsqrt(jnp.mean(wide_state * wide_state, axis=1, keepdims=True) + EPS)
        normed = (wide_state * inv_rms * gain_row).astype(jnp.bfloat16)
        logits = jnp.dot(normed, router_mat, preferred_element_type=jnp.float32)
        scores = jax.nn.sigmoid(jnp.take_along_axis(logits, chosen_ids, axis=1))
        weights = scores / jnp.sum(scores, axis=1, keepdims=True)
        flat_ids = chosen_ids.reshape(-1)
        onehot = (flat_ids[:, None] == expert_ids[None, :]).astype(jnp.int32)
        slot_rank = jnp.sum((jnp.cumsum(onehot, axis=0) - onehot) * onehot, axis=1)
        target = flat_ids * capacity + slot_rank
        selector = (target[None, :] == slot_ids[:, None]) & active
        by_token = jnp.sum(
            selector.reshape(slot_count, tok_rows, top_count).astype(jnp.int32), axis=2
        )
        buffer = jnp.dot(
            by_token.astype(jnp.bfloat16), normed, preferred_element_type=jnp.float32
        ).astype(jnp.bfloat16)
        live_slots = jnp.sum(by_token, axis=1).reshape(experts, capacity)
        slot_buffer = buffer.reshape(experts, capacity, model_width)
        slot_rows = lax.all_to_all(slot_buffer, "dp", split_axis=0, concat_axis=0, tiled=True)
        slot_live = lax.all_to_all(live_slots, "dp", split_axis=0, concat_axis=0, tiled=True)
        source_count, item_count = slot_live.shape
        row_count = source_count * item_count
        run_flat_rows = slot_rows.reshape(row_count, model_width)
        live_flat = slot_live.reshape(row_count)
        expert_out = lax.cond(jnp.any(live_flat > 0), compute_all, skip_all, run_flat_rows)
        expert_out = expert_out.reshape(source_count, item_count, model_width)
        returned = lax.all_to_all(expert_out, "dp", split_axis=0, concat_axis=0, tiled=True)
        copies = returned.reshape(slot_count, model_width)[target].reshape(
            tok_rows, top_count, model_width
        )
        mixed = jnp.einsum("tk,tkd->td", weights, copies.astype(jnp.float32))
        layer_out = (wide_state + mixed).astype(jnp.bfloat16)
        previous = lax.dynamic_index_in_dim(states, micro_index, 0, keepdims=False)
        states = lax.dynamic_update_index_in_dim(
            states, jnp.where(active, layer_out, previous), micro_index, 0
        )
        inbound = shifted(layer_out, "section", 1)
    return states[None]


HALF = 64
LANES = 2 * HALF
SLICE = 512
STRIDE = 3
MESH = pl.DeviceIdType.MESH


def relay_kernel(
    sections, line, chunks, rows,
    x_ref, route_ref, gain_ref, router_ref, gate_hbm, up_hbm, down_hbm, out_ref,
    gate_v, up_v, down_v, state, gathered, part, peer_part, relay, hidden, total,
    w_sem, x_send, x_recv, ag_send, ag_recv, ex_send, ex_recv, rs_send, rs_recv,
):
    sec = lax.axis_index("section")
    dpi = lax.axis_index("dp")
    z = dpi // 2
    core = dpi % 2
    width = x_ref.shape[1]
    ff = gate_v.shape[1]
    pieces = width // SLICE
    last = line - 1
    has_left, has_right = z > 0, z < last

    partner = (sec, z * 2 + 1 - core)
    right = (sec, jnp.minimum(dpi + 2, 2 * line - 1))
    left = (sec, jnp.maximum(dpi - 2, 0))
    after = (jnp.minimum(sec + 1, sections - 1), dpi)
    before = (jnp.maximum(sec - 1, 0), dpi)

    def span(j):
        return pl.ds(pl.multiple_of(j * rows, rows), rows)

    def ag_copy(kind, j, src):
        block = gathered.at[j, core, src]
        return pltpu.make_async_remote_copy(
            block, block, ag_send.at[j, kind, src], ag_recv.at[j, core, src],
            device_id=(right, left, partner)[kind], device_id_type=MESH,
        )

    def ag_arrival(j, which, src):
        block = gathered.at[j, which, src]
        pltpu.make_async_remote_copy(
            block, block, ag_send.at[j, 0, src], ag_recv.at[j, which, src],
            device_id=partner, device_id_type=MESH,
        ).wait_recv()

    def ex_copy(j, piece):
        cols = pl.ds(piece * SLICE, SLICE)
        return pltpu.make_async_remote_copy(
            part.at[j, 1 - core, :, :, cols], peer_part.at[j, :, :, cols],
            ex_send.at[j, piece], ex_recv.at[j, piece],
            device_id=partner, device_id_type=MESH,
        )

    def rs_copy(way, j, dest):
        block = relay.at[j, way, dest]
        return pltpu.make_async_remote_copy(
            block, block, rs_send.at[j, way, dest], rs_recv.at[j, way, dest],
            device_id=(right, left)[way], device_id_type=MESH,
        )

    def x_copy(j):
        return pltpu.make_async_remote_copy(
            out_ref.at[span(j)], state.at[j], x_send.at[j], x_recv.at[j],
            device_id=after, device_id_type=MESH,
        )

    weight_copies = [
        pltpu.make_async_copy(gate_hbm, gate_v, w_sem.at[0]),
        pltpu.make_async_copy(up_hbm, up_v, w_sem.at[1]),
        pltpu.make_async_copy(down_hbm, down_v, w_sem.at[2]),
    ]
    for copy in weight_copies:
        copy.start()

    barrier = pltpu.get_barrier_semaphore()
    neighbours = (
        (None, partner),
        (has_left, left),
        (has_right, right),
        (sec > 0, before),
        (sec < sections - 1, after),
    )
    for cond, device in neighbours:
        def greet(device=device):
            pl.semaphore_signal(barrier, inc=1, device_id=device, device_id_type=MESH)
        if cond is None:
            greet()
        else:
            pl.when(cond)(greet)
    peers = 1
    for cond, _ in neighbours[1:]:
        peers += jnp.where(cond, 1, 0)
    pl.semaphore_wait(barrier, peers)

    def enter(j):
        @pl.when(sec == 0)
        def _():
            state[j] = x_ref[span(j)]

        @pl.when(sec > 0)
        def _():
            x_copy(j).wait_recv()

        wide = state[j].astype(jnp.float32)
        inv_rms = lax.rsqrt(jnp.mean(wide * wide, axis=1, keepdims=True) + EPS)
        normed = (wide * inv_rms * gain_ref[...].astype(jnp.float32)).astype(jnp.bfloat16)
        logits = jnp.dot(normed, router_ref[...], preferred_element_type=jnp.float32)
        lane = lax.broadcasted_iota(jnp.int32, (rows, LANES), 1)
        folded = jnp.where(lane < HALF, lane, lane - HALF)
        chosen = route_ref[span(j)]
        named = folded == chosen[:, 0:1]
        for k in range(1, chosen.shape[1]):
            named = named | (folded == chosen[:, k:k + 1])
        scores = jnp.where(named, jax.nn.sigmoid(logits), 0.0)
        norm = jnp.sum(jnp.where(lane < HALF, scores, 0.0), axis=1, keepdims=True)
        weights = scores / norm
        high = weights.astype(jnp.bfloat16).astype(jnp.float32)
        carried = jnp.where(lane < HALF, high, weights - high)
        gathered[j, core, z, :, 0:width] = normed
        gathered[j, core, z, :, width:width + LANES] = carried.astype(jnp.bfloat16)

        @pl.when(has_right)
        def _():
            ag_copy(0, j, z).start()

        @pl.when(has_left)
        def _():
            ag_copy(1, j, z).start()

        ag_copy(2, j, z).start()

    def gather_hop(hop, j):
        @pl.when(z >= hop)
        def _():
            ag_arrival(j, core, z - hop)

            @pl.when(has_right)
            def _():
                ag_copy(0, j, z - hop).start()

            ag_copy(2, j, z - hop).start()

        @pl.when(z + hop <= last)
        def _():
            ag_arrival(j, core, z + hop)

            @pl.when(has_left)
            def _():
                ag_copy(1, j, z + hop).start()

            ag_copy(2, j, z + hop).start()

    def compute(j):
        for src in range(line):
            ag_arrival(j, 1 - core, src)
        count = 2 * line * rows
        block = gathered[j, :, :, :, 0:width].reshape(count, width)
        carried = gathered[j, :, :, :, width:width + LANES].reshape(count, LANES).astype(jnp.float32)
        lane = lax.broadcasted_iota(jnp.int32, (count, LANES), 1)
        mine = (lane == dpi) | (lane == dpi + HALF)
        weight = jnp.sum(jnp.where(mine, carried, 0.0), axis=1, keepdims=True)
        step = 256
        for lo in range(0, ff, step):
            cols = slice(lo, lo + step)
            gate = jnp.dot(block, gate_v[:, cols], preferred_element_type=jnp.float32)
            up = jnp.dot(block, up_v[:, cols], preferred_element_type=jnp.float32)
            hidden[:, cols] = (jax.nn.silu(gate) * up * weight).astype(jnp.bfloat16)
        for piece in range(pieces):
            cols = slice(piece * SLICE, piece * SLICE + SLICE)
            done = jnp.dot(hidden[...], down_v[:, cols], preferred_element_type=jnp.float32)
            part[j, :, :, :, cols] = done.astype(jnp.bfloat16).reshape(2, line, rows, SLICE)
            ex_copy(j, piece).start()

    def pair_sum(j, dest):
        return part[j, core, dest].astype(jnp.float32) + peer_part[j, dest].astype(jnp.float32)

    def reduce_hop(hop, j):
        for way in range(2):
            place = z if way == 0 else last - z
            dest = z + line - hop if way == 0 else z - line + hop

            @pl.when(place <= hop - 1)
            def _():
                @pl.when(place == 0)
                def _():
                    relay[j, way, dest] = pair_sum(j, dest).astype(jnp.bfloat16)

                @pl.when(place > 0)
                def _():
                    rs_copy(way, j, dest).wait_recv()
                    held = relay[j, way, dest].astype(jnp.float32)
                    relay[j, way, dest] = (pair_sum(j, dest) + held).astype(jnp.bfloat16)

                rs_copy(way, j, dest).start()

    def leave(j):
        total[...] = state[j].astype(jnp.float32) + pair_sum(j, z)

        @pl.when(has_left)
        def _():
            rs_copy(0, j, z).wait_recv()
            total[...] += relay[j, 0, z].astype(jnp.float32)

        @pl.when(has_right)
        def _():
            rs_copy(1, j, z).wait_recv()
            total[...] += relay[j, 1, z].astype(jnp.float32)

        out_ref[span(j)] = total[...].astype(jnp.bfloat16)

        @pl.when(sec < sections - 1)
        def _():
            x_copy(j).start()

    def settle(j):
        for src in range(line):
            @pl.when(has_right & (src <= z))
            def _():
                ag_copy(0, j, src).wait_send()

            @pl.when(has_left & (src >= z))
            def _():
                ag_copy(1, j, src).wait_send()

            ag_copy(2, j, src).wait_send()

            @pl.when(has_right & (src > z))
            def _():
                rs_copy(0, j, src).wait_send()

            @pl.when(has_left & (src < z))
            def _():
                rs_copy(1, j, src).wait_send()

        for piece in range(pieces):
            ex_copy(j, piece).wait_send()

        @pl.when(sec < sections - 1)
        def _():
            x_copy(j).wait_send()

    depth = 2 * line - 1

    def round_step(r, carry):
        def phase(late, work):
            past = r - late
            j = past // STRIDE

            @pl.when((past >= 0) & (past % STRIDE == 0) & (j < chunks))
            def _():
                work(j)

        def reduce_first(j):
            for piece in range(pieces):
                ex_copy(j, piece).wait_recv()
            reduce_hop(1, j)

        phase(depth, leave)
        for hop in range(last, 0, -1):
            phase(hop, functools.partial(gather_hop, hop))
        for hop in range(last, 1, -1):
            phase(last + hop, functools.partial(reduce_hop, hop))
        phase(last + 1, reduce_first)
        phase(0, enter)

        @pl.when(r == last)
        def _():
            for copy in weight_copies:
                copy.wait()

        phase(last, compute)
        phase(depth + 2, settle)
        return carry

    lax.fori_loop(0, (chunks - 1) * STRIDE + depth + 3, round_step, 0)


def on_device_dense(shape, inputs, route, gain, router, w_gate, w_up, w_down):
    sections = shape["section"]
    line = shape["dp"] // 2
    micro_count, tok_rows, width = inputs.shape
    top = route.shape[-1]
    experts = router.shape[-1]
    ff = w_gate.shape[-1]
    rows = min(ROWS, tok_rows)
    token_rows = micro_count * tok_rows
    chunks = token_rows // rows
    padded = jnp.pad(router[0], ((0, 0), (0, HALF - experts)))
    router_mat = jnp.concatenate([padded, padded], axis=1)
    bf16 = jnp.bfloat16
    count = 2 * line * rows
    dma = pltpu.SemaphoreType.DMA
    vmem = pl.BlockSpec(memory_space=pltpu.VMEM)
    far = pl.BlockSpec(memory_space=pl.ANY)
    flops = 6 * chunks * count * width * ff
    result = pl.pallas_call(
        functools.partial(relay_kernel, sections, line, chunks, rows),
        out_shape=jax.ShapeDtypeStruct((token_rows, width), bf16),
        in_specs=[vmem] * 4 + [far] * 3,
        out_specs=vmem,
        scratch_shapes=[
            pltpu.VMEM((width, ff), bf16),
            pltpu.VMEM((width, ff), bf16),
            pltpu.VMEM((ff, width), bf16),
            pltpu.VMEM((chunks, rows, width), bf16),
            pltpu.VMEM((chunks, 2, line, rows, width + LANES), bf16),
            pltpu.VMEM((chunks, 2, line, rows, width), bf16),
            pltpu.VMEM((chunks, line, rows, width), bf16),
            pltpu.VMEM((chunks, 2, line, rows, width), bf16),
            pltpu.VMEM((count, ff), bf16),
            pltpu.VMEM((rows, width), jnp.float32),
            dma((3,)),
            dma((chunks,)),
            dma((chunks,)),
            dma((chunks, 3, line)),
            dma((chunks, 2, line)),
            dma((chunks, width // SLICE)),
            dma((chunks, width // SLICE)),
            dma((chunks, 2, line)),
            dma((chunks, 2, line)),
        ],
        compiler_params=pltpu.CompilerParams(
            collective_id=0, has_side_effects=True, vmem_limit_bytes=56 * 2**20
        ),
        cost_estimate=pl.CostEstimate(
            flops=flops, bytes_accessed=6 * width * ff, transcendentals=chunks * count * ff
        ),
    )(
        inputs.reshape(token_rows, width),
        route.reshape(token_rows, top),
        gain,
        router_mat,
        w_gate[0, 0],
        w_up[0, 0],
        w_down[0, 0],
    )
    return result.reshape(1, micro_count, tok_rows, width)


ROWS = 16


def on_device(shape, inputs, route, gain, router, w_gate, w_up, w_down):
    tok_rows = inputs.shape[1]
    experts = router.shape[-1]
    args = (inputs, route, gain, router, w_gate, w_up, w_down)
    if 2 * tok_rows * route.shape[-1] // experts >= tok_rows and experts <= HALF:
        return on_device_dense(shape, *args)
    return on_device_sparse(*args)


def solution(mesh):
    body = functools.partial(on_device, dict(mesh.shape))
    in_specs = (
        P(None, "dp", None),
        P("section", None, "dp", None),
        P("section", None),
        P("section", None, None),
        P("section", "dp", None, None),
        P("section", "dp", None, None),
        P("section", "dp", None, None),
    )
    out_specs = P("section", None, "dp", None)
    return jax.shard_map(
        body, mesh=mesh, in_specs=in_specs, out_specs=out_specs, check_vma=False
    )
```
